128 devices in a mesh: row: 8 (over y_lo, x), col: 16 (over z, y_hi, core).
Axes of the slice: x: 4, y: 4 (y_hi: 2, y_lo: 2; y = y_hi * 2 + y_lo), z: 4, core: 2. Of those that a mesh axis runs over, the one named last changes fastest.
Arguments:
- amplitudes: float32 [16, 3, 1024, 1024], P('row', None, 'col'), may hold values from -6 to 6
- dressing: float32 [1024, 1024], replicated, may hold values from -0.1875 to 0.1875
- integrals: float32 [1024, 3, 16384], P('row', None, 'col'), may hold values from -0.109375 to 0.109375
- occupied_energy: float32 [128], replicated, may hold values from -2 to -0.3
- virtual_energy: float32 [1024], replicated, may hold values from 0.2 to 3
- occupied_rows: int32 [16], P('row'), may hold values from 0 to 127
- virtual_rows: int32 [1024], replicated, may hold values from 0 to 1023
- occupied_columns: int32 [16], P('col'), may hold values from 0 to 127
- virtual_columns: int32 [1024], replicated, may hold values from 0 to 1023
Outputs:
- residual: float32 [16384, 16384], P('row', 'col')
The draws below stay inside these ranges and needn't reach their ends.
All inputs are finite; a program needn't handle non-finite values.
Results may differ from the reference program's by a relative error of at most 0.00007.
Values sent between devices are 32-bit elements; how exact they have to be, the bound alone decides.
A program may use at most 128 MiB of HBM per device.

```python
import jax
import jax.numpy as jnp
from jax import lax

NV = 1024
NA = 1024
NB = 1024
NOCC = 128
NK = 3
NI = 16
NJ = 16


def touch_ends(entries, key, smallest, high):
    longest = entries.shape.index(max(entries.shape))
    spots = []
    for shift in (0, 1):
        where = [jax.random.randint(jax.random.fold_in(key, axis), (), 0, length) for axis, length in enumerate(entries.shape)]
        where[longest] = (where[longest] + shift) % entries.shape[longest]
        spots.append(tuple(where))
    return entries.at[spots[0]].set(smallest).at[spots[1]].set(high)


def steps_of(own_key, dims, shards, smallest, largest):
    def one(axis_at, shards_of):
        draws = jax.random.uniform(jax.random.fold_in(jax.random.fold_in(own_key, 6), axis_at), (shards_of,), jnp.float32, smallest / len(shards), largest / len(shards))
        return jnp.repeat(jnp.exp(draws), dims[axis_at] // shards_of).reshape((-1,) + (1,) * (len(dims) - axis_at - 1))

    gain = one(*shards[0])
    for cut in shards[1:]:
        gain = gain * one(*cut)
    return gain


def gaussian(rng, dims, width, limit, split=(), dtype=jnp.bfloat16):
    array = width * jax.random.normal(rng, dims, jnp.float32)
    if split:
        array = array * steps_of(rng, dims, split, -0.22, 0.18)
    return jnp.clip(array, -limit, limit).astype(dtype)


def setup_inputs(seed: int = 0) -> dict:
    arg_keys = jax.random.split(jax.random.key(seed), 10)
    return {
        "amplitudes": gaussian(arg_keys[0], (NI, NK, NA, NV), 1.0, 6.0, ((0, 8), (2, 16)), jnp.float32),
        "dressing": gaussian(arg_keys[1], (NV, NV), NV ** -0.5, 0.1875, (), jnp.float32),
        "integrals": gaussian(arg_keys[2], (NV, NK, NJ * NB), (NK * NV) ** -0.5, 0.109375, ((0, 8), (2, 16)), jnp.float32),
        "occupied_energy": jnp.clip(jax.random.uniform(arg_keys[3], (NOCC,), jnp.float32, -2.0, -0.3), -2.0, -0.3),
        "virtual_energy": jnp.clip(jax.random.uniform(arg_keys[4], (NV,), jnp.float32, 0.2, 3.0), 0.2, 3.0),
        "occupied_rows": touch_ends(jax.random.randint(arg_keys[5], (NI,), 0, NOCC), jax.random.fold_in(arg_keys[5], 1), 0, NOCC - 1).astype(jnp.int32),
        "virtual_rows": touch_ends(jax.random.randint(arg_keys[6], (NA,), 0, NV), jax.random.fold_in(arg_keys[6], 1), 0, NV - 1).astype(jnp.int32),
        "occupied_columns": touch_ends(jax.random.randint(arg_keys[7], (NJ,), 0, NOCC), jax.random.fold_in(arg_keys[7], 1), 0, NOCC - 1).astype(jnp.int32),
        "virtual_columns": touch_ends(jax.random.randint(arg_keys[8], (NB,), 0, NV), jax.random.fold_in(arg_keys[8], 1), 0, NV - 1).astype(jnp.int32),
    }


def reference(amplitudes, dressing, integrals, occupied_energy, virtual_energy, occupied_rows, virtual_rows, occupied_columns, virtual_columns):
    dressed = jnp.dot(amplitudes.reshape(-1, NV), dressing, precision=lax.Precision.HIGHEST).reshape(amplitudes.shape)
    energy_a = virtual_energy[virtual_rows]
    energy_b = virtual_energy[virtual_columns]
    energy_i = occupied_energy[occupied_rows]
    energy_j = occupied_energy[occupied_columns]

    def one_row(inputs):
        block, level = inputs
        contracted = jnp.einsum("kac,ckj->aj", block, integrals, precision=lax.Precision.HIGHEST)
        denominator = (energy_a[:, None, None] + energy_b[None, None, :]) - level - energy_j[None, :, None]
        return contracted / denominator.reshape(NA, NJ * NB)

    result = lax.map(one_row, (dressed, energy_i))
    return result.reshape(NI * NA, NJ * NB)
```

```python
import functools

import jax
import jax.numpy as jnp
from jax import lax
from jax.experimental import pallas as pl
from jax.experimental.pallas import tpu as pltpu
from jax.sharding import PartitionSpec as P

MESH = pl.DeviceIdType.MESH
BF16, F32 = jnp.bfloat16, jnp.float32
PIECE = 64
BALANCED_W, BALANCED_A = (1,), (1,)


def parts(values):
    high = values.astype(BF16)
    return high, (values - high.astype(F32)).astype(BF16)


def dot(a, b):
    return jnp.dot(a, b, preferred_element_type=F32)


def dot3(a, b_high, b_low):
    a_high, a_low = parts(a)
    return dot(a_high, b_high) + dot(a_high, b_low) + dot(a_low, b_high)


def column(row):
    tiles = [
        jnp.transpose(jnp.broadcast_to(row[:, at : at + 128], (128, 128)))
        for at in range(0, row.shape[1], 128)
    ]
    return jnp.concatenate(tiles, axis=0)


def kernel(
    amp,
    dressing,
    w_in,
    occupied_energy,
    virtual_energy,
    occupied_rows,
    virtual_rows,
    occupied_columns,
    virtual_columns,
    out,
    A,
    W,
    SH,
    SL,
    C,
    EA,
    EB,
    EI,
    send_sem,
    recv_w,
    recv_a,
    local_sem,
    out_sem,
):
    row, col = lax.axis_index("row"), lax.axis_index("col")
    x, ylo = row % 4, row // 4
    z, yhi, core = col // 4, (col // 2) % 2, col % 2

    def source_row(dx, dy):
        return ((ylo + dy) % 2) * 4 + (x + dx) % 4

    def source_col(dz, dy, dcore):
        return ((z + dz) % 4) * 4 + ((yhi + dy) % 2) * 2 + (core + dcore) % 2

    xp, xm, yl = (source_row(1, 0), col), (source_row(3, 0), col), (source_row(0, 1), col)
    zp, zm = (row, source_col(1, 0, 0)), (row, source_col(3, 0, 0))
    yh, sib = (row, source_col(0, 1, 0)), (row, source_col(0, 0, 1))
    neighbours = (xp, xm, yl, zp, zm, yh, sib)

    def rows_w(r, h):
        return pl.ds(pl.multiple_of(r * 128 + h * PIECE, PIECE), PIECE)

    def rows_a(s):
        return pl.ds(pl.multiple_of(s * PIECE, PIECE), PIECE)

    counts = [0, 0, 0]

    def copy_w(k, r, h, target, own=False):
        return pltpu.make_async_remote_copy(
            src_ref=w_in.at[k, pl.ds(h * PIECE, PIECE)] if own else W.at[k, rows_w(r, h)],
            dst_ref=W.at[k, rows_w(r, h)],
            send_sem=send_sem.at[k],
            recv_sem=recv_w.at[k, 2 * r + h],
            device_id=target,
            device_id_type=MESH,
        )

    def copy_a(k, i, s, target):
        return pltpu.make_async_remote_copy(
            src_ref=A.at[k, i, rows_a(s)],
            dst_ref=A.at[k, i, rows_a(s)],
            send_sem=send_sem.at[k],
            recv_sem=recv_a.at[k, i, s],
            device_id=target,
            device_id_type=MESH,
        )

    def send_w(k, r, h, *targets, own=False):
        for target in targets:
            copy_w(k, r, h, target, own).start()
            counts[k] += 1

    def send_a(k, i, s, *targets):
        for target in targets:
            copy_a(k, i, s, target).start()
            counts[k] += 1

    def wait_w(k, r, h):
        copy_w(k, r, h, yl).wait_recv()

    def wait_a(k, i, s):
        copy_a(k, i, s, sib).wait_recv()

    own_w, own_a = source_row(0, 0), source_col(0, 0, 0)

    def start_w(k):
        for first in (0, 1):
            send_w(k, own_w, first, xp, own=True)
            send_w(k, own_w, 1 - first, xm, own=True)
            send_w(k, own_w, first, yl, own=True)

    def start_a(k):
        for first in (0, 1):
            send_a(k, first, own_a, zp)
            send_a(k, 1 - first, own_a, zm)
            send_a(k, first, own_a, yh, sib)

    def pass_first(k, dy):
        on_w = dy == 0 or k not in BALANCED_W
        on_a = dy == 0 or k not in BALANCED_A
        behind, ahead = source_row(3, dy), source_row(1, dy)
        below, above = source_col(3, dy, 0), source_col(1, dy, 0)
        if on_w:
            wait_w(k, behind, 0)
            send_w(k, behind, 0, xp)
            wait_w(k, ahead, 1)
            send_w(k, ahead, 1, xm)
        wait_a(k, 0, below)
        send_a(k, 0, below, *((zp,) if on_a else ()), sib)
        wait_a(k, 1, above)
        send_a(k, 1, above, *((zm,) if on_a else ()), sib)
        wait_a(k, 1, below)
        send_a(k, 1, below, sib)
        wait_a(k, 0, above)
        send_a(k, 0, above, sib)

    def pass_partner(k):
        theirs_w, theirs_a = source_row(0, 1), source_col(0, 1, 0)
        for h in (0, 1):
            wait_w(k, theirs_w, h)
            send_w(k, theirs_w, h, *((xp, xm) if h == 0 else (xm, xp)))
            wait_a(k, h, theirs_a)
            send_a(k, h, theirs_a, *((zp, zm) if h == 0 else (zm, zp)), sib)

    def pass_far(k, dy):
        far_w, far_a = source_row(2, dy), source_col(2, dy, 0)
        for h in (0, 1):
            if dy == 0 and k in BALANCED_W:
                wait_w(k, far_w, h)
                send_w(k, far_w, h, yl)
            wait_a(k, h, far_a)
            send_a(k, h, far_a, *((yh,) if dy == 0 and k in BALANCED_A else ()), sib)

    def rest_w(k, dy):
        on_w = dy == 0 or k not in BALANCED_W
        behind, ahead = source_row(3, dy), source_row(1, dy)
        if not on_w:
            wait_w(k, behind, 0)
            wait_w(k, ahead, 1)
        wait_w(k, behind, 1)
        wait_w(k, ahead, 0)
        if dy == 1 or k not in BALANCED_W:
            for h in (0, 1):
                wait_w(k, source_row(2, dy), h)

    def rest_a(k, dy, steps=(0, 1, 3, 2)):
        for dz in steps:
            for i in (0, 1):
                wait_a(k, i, source_col(dz, dy, 1))

    def split(source, slot, first, count):
        def one(step, _):
            rows = pl.ds(pl.multiple_of(first + step * 64, 64), 64)
            high, low = parts(source[rows])
            SH[slot, rows] = high
            SL[slot, rows] = low
            return 0

        lax.fori_loop(0, count // 64, one, 0)

    def product(k, slot, group, depth_at, depth):
        rows = pl.ds(pl.multiple_of(group * 128, 128), 128)
        if depth == 1024:
            inner = slice(None)
        else:
            inner = pl.ds(pl.multiple_of(depth_at, depth), depth)
        a = A[k, :, rows, inner].reshape(256, depth)
        value = dot3(a, SH[slot, inner], SL[slot, inner])
        return rows, value.reshape(2, 128, 1024)

    def accumulate(k, slot, group, depth_at=0, depth=1024):
        rows, value = product(k, slot, group, depth_at, depth)
        if k == 0:
            C[:, rows] = value
        else:
            C[:, rows] += value

    def out_copy(group):
        rows = pl.ds(pl.multiple_of(group * 128, 128), 128)
        return pltpu.make_async_copy(C.at[:, rows], out.at[:, rows], out_sem.at[group])

    def finish(k, slot, group, depth_at=0, depth=1024):
        rows, value = product(k, slot, group, depth_at, depth)
        sums = jnp.concatenate([EA[rows]] * 8, axis=1) + EB[0:1, :]
        level_j = EI[2:3, 0:1]
        for i in (0, 1):
            denominator = (sums - EI[i : i + 1, 0:1]) - level_j
            C[i, rows] = (C[i, rows] + value[i]) / denominator
        out_copy(group).start()

    def groups(first, last, body):
        def one(group, _):
            body(group)
            return 0

        lax.fori_loop(first, last, one, 0)

    chunk = 256
    loads = [
        pltpu.make_async_copy(
            dressing.at[pl.ds(at, chunk)], C.at[0, pl.ds(at, chunk)], local_sem.at[at // chunk]
        )
        for at in range(0, 1024, chunk)
    ]
    amp_loads = [
        pltpu.make_async_copy(amp.at[:, k], A.at[k, :, rows_a(own_a)], local_sem.at[4 + k])
        for k in range(3)
    ]
    w_load = pltpu.make_async_copy(
        w_in, W.at[:, pl.ds(pl.multiple_of(own_w * 128, 128), 128)], local_sem.at[7]
    )
    for load in (*loads, *amp_loads, w_load):
        load.start()
    barrier = pltpu.get_barrier_semaphore()
    for target in neighbours:
        pl.semaphore_signal(barrier, inc=1, device_id=target, device_id_type=MESH)
    pl.semaphore_wait(barrier, len(neighbours))
    start_w(0)

    for number, load in enumerate(loads):
        load.wait()
        split(C.at[0], 1, number * chunk, chunk)
    for load in amp_loads:
        load.wait()

    def dress(k):
        dressed = dot3(A[k, :, rows_a(own_a)].reshape(128, 1024), SH[1], SL[1])
        A[k, :, rows_a(own_a)] = dressed.reshape(2, PIECE, 1024)

    dress(0)
    start_a(0)
    dress(1)
    dress(2)
    w_load.wait()

    table = virtual_energy[...]
    lanes = lax.broadcasted_iota(jnp.int32, (128, 1024), 1)
    for at in range(0, 1024, 128):
        index = column(virtual_rows[:, at : at + 128])
        index = jnp.concatenate([index] * 8, axis=1)
        found = jnp.sum(jnp.where(index == lanes, table, 0.0), axis=1, keepdims=True)
        EA[at : at + 128] = jnp.broadcast_to(found, (128, 128))
        index = column(virtual_columns[:, at : at + 128])
        index = jnp.concatenate([index] * 8, axis=1)
        found = jnp.sum(jnp.where(index == lanes, table, 0.0), axis=1, keepdims=True)
        found = jnp.transpose(jnp.broadcast_to(found, (128, 128)))
        EB[:, at : at + 128] = found[:8]
    places = lax.broadcasted_iota(jnp.int32, (1, 128), 1)
    levels = (occupied_rows[0], occupied_rows[1], occupied_columns[0])
    for number, place in enumerate(levels):
        level = jnp.sum(
            jnp.where(places == place, occupied_energy[...], 0.0), axis=1, keepdims=True
        )
        EI[number : number + 1] = jnp.broadcast_to(level, (1, 128))

    pass_first(0, 0)
    pass_partner(0)
    start_w(1)
    start_a(1)
    pass_far(0, 0)
    pass_first(0, 1)
    pass_far(0, 1)

    for k in (1, 2):
        for dy in (0, 1):
            rest_w(k - 1, dy)
            rest_a(k - 1, dy)
        slot = (k - 1) % 2
        split(W.at[k - 1], slot, 0, 1024)
        groups(0, 4, functools.partial(accumulate, k - 1, slot))
        pass_first(k, 0)
        groups(4, 8, functools.partial(accumulate, k - 1, slot))
        pass_partner(k)
        if k == 1:
            start_w(2)
            start_a(2)
            pass_far(k, 0)
            pass_first(k, 1)
            pass_far(k, 1)
    pass_far(2, 0)

    ours, theirs = ylo * 512, (1 - ylo) * 512
    rest_w(2, 0)
    rest_a(2, 0)
    split(W.at[2], 0, ours, 512)
    groups(0, 4, lambda n: accumulate(2, 0, 2 * n + yhi, ours, 512))
    pass_first(2, 1)
    rest_a(2, 1, (0, 1, 3))
    other = 1 - yhi
    for dz in (0, 1, 3):
        accumulate(2, 0, ((z + dz) % 4) * 2 + other, ours, 512)
    pass_far(2, 1)
    rest_w(2, 1)
    split(W.at[2], 0, theirs, 512)
    groups(0, 4, lambda n: finish(2, 0, 2 * n + yhi, theirs, 512))
    for dz in (0, 1, 3):
        finish(2, 0, ((z + dz) % 4) * 2 + other, theirs, 512)
    rest_a(2, 1, (2,))
    finish(2, 0, ((z + 2) % 4) * 2 + other)

    for k in range(3):
        share = A.at[0:2, :, pl.ds(0, counts[k] * PIECE // 4)]
        pltpu.make_async_remote_copy(
            src_ref=share,
            dst_ref=share,
            send_sem=send_sem.at[k],
            recv_sem=recv_a.at[0, 0, 0],
            device_id=sib,
            device_id_type=MESH,
        ).wait_send()
    for group in range(8):
        out_copy(group).wait()


def on_device(
    amplitudes,
    dressing,
    integrals,
    occupied_energy,
    virtual_energy,
    occupied_rows,
    virtual_rows,
    occupied_columns,
    virtual_columns,
):
    anywhere = pl.BlockSpec(memory_space=pl.ANY)
    vmem = pl.BlockSpec(memory_space=pltpu.VMEM)
    smem = pl.BlockSpec(memory_space=pltpu.SMEM)
    residual = pl.pallas_call(
        kernel,
        out_shape=jax.ShapeDtypeStruct((2, 1024, 1024), F32),
        in_specs=[anywhere, anywhere, anywhere, vmem, vmem, smem, vmem, smem, vmem],
        out_specs=anywhere,
        scratch_shapes=[
            pltpu.VMEM((3, 2, 1024, 1024), F32),
            pltpu.VMEM((3, 1024, 1024), F32),
            pltpu.VMEM((2, 1024, 1024), BF16),
            pltpu.VMEM((2, 1024, 1024), BF16),
            pltpu.VMEM((2, 1024, 1024), F32),
            pltpu.VMEM((1024, 128), F32),
            pltpu.VMEM((8, 1024), F32),
            pltpu.VMEM((8, 128), F32),
            pltpu.SemaphoreType.DMA((3,)),
            pltpu.SemaphoreType.DMA((3, 16)),
            pltpu.SemaphoreType.DMA((3, 2, 16)),
            pltpu.SemaphoreType.DMA((8,)),
            pltpu.SemaphoreType.DMA((8,)),
        ],
        compiler_params=pltpu.CompilerParams(
            collective_id=0, has_side_effects=True, vmem_limit_bytes=58 * 2**20
        ),
        cost_estimate=pl.CostEstimate(
            flops=42_000_000_000, bytes_accessed=20_000_000, transcendentals=0
        ),
    )(
        amplitudes,
        dressing,
        jnp.transpose(integrals, (1, 0, 2)),
        occupied_energy.reshape(1, -1),
        virtual_energy.reshape(1, -1),
        occupied_rows,
        virtual_rows.reshape(1, -1),
        occupied_columns,
        virtual_columns.reshape(1, -1),
    )
    return residual.reshape(2048, 1024)


def solution(mesh):
    return jax.shard_map(
        on_device,
        mesh=mesh,
        in_specs=(
            P("row", None, "col", None),
            P(),
            P("row", None, "col"),
            P(),
            P(),
            P("row"),
            P(),
            P("col"),
            P(),
        ),
        out_specs=P("row", "col"),
        check_vma=False,
    )
```

```python
import functools

import jax
import jax.numpy as jnp
from jax import lax
from jax.experimental import pallas as pl
from jax.experimental.pallas import tpu as pltpu
from jax.sharding import PartitionSpec as P

MESH = pl.DeviceIdType.MESH
BF16, F32 = jnp.bfloat16, jnp.float32
PIECE = 64

SEND, WAIT, DRESSING, DRESS, ENERGY, SPLIT, FULL, HALF = range(8)
XP, XM, ZP, ZM, Y = range(5)
INT, AMP = range(2)
PLAN = (
    (SEND, XP, INT, 0, 0, 0, 0), (SEND, XP, INT, 0, 0, 0, 1), (SEND, XM, INT, 0, 0, 0, 1),
    (SEND, XM, INT, 0, 0, 0, 0), (SEND, Y, INT, 0, 0, 0, 0), (SEND, Y, INT, 0, 0, 0, 1),
    (SEND, Y, INT, 1, 0, 0, 0), (DRESSING,), (DRESS, 0), (SEND, XP, INT, 1, 0, 0, 0),
    (SEND, XM, INT, 1, 0, 0, 1), (SEND, ZP, AMP, 0, 0, 0, 0), (SEND, ZP, AMP, 0, 0, 0, 1),
    (SEND, ZM, AMP, 0, 0, 0, 1), (SEND, ZM, AMP, 0, 0, 0, 0), (SEND, Y, AMP, 0, 0, 0, 0), (DRESS, 1),
    (WAIT, INT, 0, 3, 0, 0), (WAIT, INT, 0, 1, 0, 1), (WAIT, INT, 0, 0, 1, 0), (DRESS, 2), (ENERGY,),
    (SEND, XP, INT, 0, 3, 0, 0), (SEND, XM, INT, 0, 1, 0, 1), (SEND, Y, AMP, 0, 0, 0, 1),
    (SEND, ZP, AMP, 1, 0, 0, 0), (SEND, ZM, AMP, 1, 0, 0, 1), (WAIT, INT, 0, 3, 0, 1),
    (WAIT, INT, 0, 1, 0, 0), (WAIT, INT, 0, 0, 1, 1), (WAIT, AMP, 0, 3, 0, 0), (WAIT, AMP, 0, 1, 0, 1),
    (SEND, XP, INT, 0, 0, 1, 0), (SEND, XM, INT, 0, 0, 1, 1), (SEND, Y, AMP, 1, 0, 0, 0),
    (SEND, ZP, AMP, 0, 3, 0, 0), (SEND, ZM, AMP, 0, 1, 0, 1), (WAIT, INT, 1, 3, 0, 0),
    (WAIT, INT, 1, 1, 0, 1), (WAIT, INT, 1, 0, 1, 0), (WAIT, AMP, 0, 3, 0, 1), (WAIT, AMP, 0, 1, 0, 0),
    (SEND, XP, INT, 0, 0, 1, 1), (SEND, XM, INT, 0, 0, 1, 0), (SEND, Y, INT, 1, 0, 0, 1),
    (SEND, ZP, AMP, 1, 0, 0, 1), (SEND, ZM, AMP, 1, 0, 0, 0), (WAIT, INT, 0, 2, 0, 0),
    (WAIT, INT, 0, 2, 0, 1), (WAIT, AMP, 0, 0, 1, 0), (SPLIT, 0, 0), (WAIT, AMP, 1, 3, 0, 0),
    (WAIT, AMP, 1, 1, 0, 1), (HALF, 0, 0, 0, 0), (HALF, 0, 1, 0, 0), (HALF, 0, 3, 0, 0),
    (SEND, XP, INT, 1, 0, 0, 1), (SEND, XM, INT, 1, 0, 0, 0), (SEND, Y, AMP, 1, 0, 0, 1),
    (SEND, ZP, AMP, 0, 0, 1, 0), (SEND, ZM, AMP, 0, 0, 1, 0), (WAIT, INT, 0, 3, 1, 0),
    (WAIT, INT, 0, 1, 1, 1), (WAIT, AMP, 0, 0, 1, 1), (WAIT, AMP, 0, 2, 0, 0), (WAIT, AMP, 0, 2, 0, 1),
    (HALF, 0, 0, 1, 0), (HALF, 0, 2, 0, 0), (SEND, XP, INT, 0, 3, 1, 0), (SEND, XM, INT, 0, 1, 1, 1),
    (SEND, Y, INT, 2, 0, 0, 0), (SEND, ZP, AMP, 0, 0, 1, 1), (SEND, ZM, AMP, 0, 0, 1, 1),
    (WAIT, INT, 0, 3, 1, 1), (WAIT, INT, 0, 1, 1, 0), (WAIT, AMP, 1, 0, 1, 0), (WAIT, AMP, 1, 3, 0, 1),
    (WAIT, AMP, 1, 1, 0, 0), (SEND, XP, INT, 1, 3, 0, 0), (SEND, XM, INT, 1, 1, 0, 1),
    (SEND, Y, AMP, 2, 0, 0, 0), (SEND, ZP, AMP, 1, 3, 0, 0), (SEND, ZM, AMP, 1, 1, 0, 1),
    (WAIT, INT, 1, 3, 0, 1), (WAIT, INT, 1, 1, 0, 0), (WAIT, INT, 1, 0, 1, 1), (WAIT, AMP, 0, 3, 1, 0),
    (WAIT, AMP, 0, 1, 1, 0), (SEND, XP, INT, 1, 0, 1, 0), (SEND, XM, INT, 1, 0, 1, 1),
    (SEND, Y, INT, 2, 0, 0, 1), (SEND, ZP, AMP, 0, 3, 1, 0), (SEND, ZM, AMP, 1, 0, 1, 0),
    (WAIT, INT, 0, 2, 1, 0), (WAIT, INT, 0, 2, 1, 1), (WAIT, AMP, 1, 0, 1, 1), (SPLIT, 0, 1),
    (WAIT, AMP, 0, 3, 1, 1), (WAIT, AMP, 0, 1, 1, 1), (HALF, 0, 0, 0, 1), (HALF, 0, 0, 1, 1), (FULL, 0, 1, 1),
    (SEND, XP, INT, 1, 0, 1, 1), (SEND, XM, INT, 1, 0, 1, 0), (SEND, Y, AMP, 2, 0, 0, 1), (FULL, 0, 3, 1),
    (WAIT, INT, 1, 2, 0, 0), (WAIT, INT, 1, 2, 0, 1), (WAIT, INT, 2, 0, 1, 0), (WAIT, AMP, 1, 2, 0, 0),
    (WAIT, AMP, 1, 2, 0, 1), (SEND, ZP, AMP, 1, 0, 1, 0), (SEND, ZM, AMP, 0, 1, 1, 1), (HALF, 0, 1, 0, 1),
    (HALF, 0, 2, 0, 1), (HALF, 0, 3, 0, 1), (SEND, XP, INT, 2, 0, 0, 0), (SEND, XM, INT, 2, 0, 0, 1),
    (SEND, Y, INT, 1, 2, 0, 0), (SPLIT, 1, 0), (WAIT, INT, 1, 3, 1, 0), (WAIT, INT, 1, 1, 1, 1),
    (WAIT, AMP, 2, 0, 1, 0), (SEND, ZP, AMP, 1, 0, 1, 1), (SEND, ZM, AMP, 1, 0, 1, 1), (HALF, 1, 0, 0, 0),
    (WAIT, AMP, 0, 2, 1, 0), (WAIT, AMP, 1, 1, 1, 0), (HALF, 1, 0, 1, 0), (HALF, 1, 1, 0, 0),
    (HALF, 1, 2, 0, 0), (SEND, XP, INT, 2, 0, 0, 1), (SEND, XM, INT, 2, 0, 0, 0), (SEND, Y, INT, 1, 2, 0, 1),
    (HALF, 1, 3, 0, 0), (WAIT, INT, 1, 3, 1, 1), (WAIT, INT, 1, 1, 1, 0), (WAIT, INT, 2, 0, 1, 1),
    (SEND, ZP, AMP, 2, 0, 0, 0), (SEND, ZM, AMP, 2, 0, 0, 1), (WAIT, AMP, 1, 3, 1, 0),
    (WAIT, AMP, 0, 2, 1, 1), (FULL, 0, 2, 1), (SEND, XP, INT, 2, 0, 1, 0), (SEND, XM, INT, 2, 0, 1, 1),
    (SEND, Y, AMP, 1, 2, 0, 0), (SEND, ZP, AMP, 2, 0, 0, 1), (SEND, ZM, AMP, 2, 0, 0, 0),
    (WAIT, INT, 2, 3, 0, 0), (WAIT, INT, 2, 1, 0, 1), (WAIT, AMP, 2, 0, 1, 1), (WAIT, AMP, 1, 3, 1, 1),
    (WAIT, AMP, 1, 1, 1, 1), (HALF, 1, 3, 1, 0), (HALF, 1, 1, 1, 0), (SEND, XP, INT, 2, 3, 0, 0),
    (SEND, XM, INT, 2, 1, 0, 1), (SEND, Y, AMP, 1, 2, 0, 1), (SEND, ZP, AMP, 2, 0, 1, 0),
    (SEND, ZM, AMP, 2, 0, 1, 1), (WAIT, INT, 2, 3, 0, 1), (WAIT, INT, 2, 1, 0, 0), (WAIT, INT, 1, 2, 1, 0),
    (WAIT, AMP, 2, 3, 0, 0), (WAIT, AMP, 2, 1, 0, 1), (SEND, XP, INT, 2, 0, 1, 1),
    (SEND, XM, INT, 2, 0, 1, 0), (SEND, ZP, AMP, 2, 3, 0, 0), (SEND, ZM, AMP, 2, 1, 0, 1),
    (WAIT, INT, 2, 3, 1, 0), (WAIT, INT, 2, 1, 1, 1), (WAIT, INT, 1, 2, 1, 1), (SPLIT, 1, 1),
    (WAIT, AMP, 2, 3, 0, 1), (WAIT, AMP, 2, 1, 0, 0), (HALF, 1, 0, 0, 1), (HALF, 1, 0, 1, 1),
    (HALF, 1, 1, 0, 1), (HALF, 1, 1, 1, 1), (SEND, XP, INT, 2, 3, 1, 0), (SEND, XM, INT, 2, 1, 1, 1),
    (SEND, ZP, AMP, 2, 0, 1, 1), (SEND, ZM, AMP, 2, 0, 1, 0), (HALF, 1, 2, 0, 1), (WAIT, INT, 2, 2, 0, 0),
    (WAIT, INT, 2, 2, 0, 1), (WAIT, AMP, 1, 2, 1, 0), (WAIT, AMP, 2, 3, 1, 0), (WAIT, AMP, 2, 1, 1, 1),
    (HALF, 1, 3, 0, 1), (HALF, 1, 3, 1, 1), (SPLIT, 2, 0), (HALF, 2, 0, 0, 0), (SEND, ZP, AMP, 2, 3, 1, 0),
    (SEND, ZM, AMP, 2, 1, 1, 1), (HALF, 2, 0, 1, 0), (WAIT, INT, 2, 3, 1, 1), (WAIT, INT, 2, 1, 1, 0),
    (WAIT, AMP, 1, 2, 1, 1), (WAIT, AMP, 2, 2, 0, 0), (WAIT, AMP, 2, 2, 0, 1), (HALF, 2, 1, 0, 0),
    (HALF, 2, 3, 0, 0), (FULL, 1, 2, 1), (HALF, 2, 2, 0, 0), (WAIT, INT, 2, 2, 1, 0), (WAIT, INT, 2, 2, 1, 1),
    (SPLIT, 2, 1), (WAIT, AMP, 2, 3, 1, 1), (WAIT, AMP, 2, 1, 1, 0), (HALF, 2, 0, 0, 1), (HALF, 2, 0, 1, 1),
    (FULL, 2, 1, 1), (FULL, 2, 3, 1), (WAIT, AMP, 2, 2, 1, 0), (WAIT, AMP, 2, 2, 1, 1), (HALF, 2, 1, 0, 1),
    (HALF, 2, 2, 0, 1), (FULL, 2, 2, 1), (HALF, 2, 3, 0, 1),
)


def parts(values):
    high = values.astype(BF16)
    return high, (values - high.astype(F32)).astype(BF16)


def dot(a, b):
    return jnp.dot(a, b, preferred_element_type=F32)


def dot3(a, b_high, b_low):
    a_high, a_low = parts(a)
    return dot(a_high, b_high) + dot(a_high, b_low) + dot(a_low, b_high)


def column(row):
    tiles = [
        jnp.transpose(jnp.broadcast_to(row[:, at : at + 128], (128, 128)))
        for at in range(0, row.shape[1], 128)
    ]
    return jnp.concatenate(tiles, axis=0)


def kernel(
    amp,
    dressing,
    w_in,
    occupied_energy,
    virtual_energy,
    occupied_rows,
    virtual_rows,
    occupied_columns,
    virtual_columns,
    C,
    A,
    W,
    SH,
    SL,
    EA,
    EB,
    EI,
    send_sem,
    recv_w,
    recv_a,
    local_sem,
    out_sem,
):
    row, col = lax.axis_index("row"), lax.axis_index("col")
    x, ylo = row % 4, row // 4
    z, yhi, core = col // 4, (col // 2) % 2, col % 2

    def source_row(dx, dy):
        return ((ylo + dy) % 2) * 4 + (x + dx) % 4

    def source_col(dz, dy, dcore):
        return ((z + dz) % 4) * 4 + ((yhi + dy) % 2) * 2 + (core + dcore) % 2

    xp, xm, yl = (source_row(1, 0), col), (source_row(3, 0), col), (source_row(0, 1), col)
    zp, zm = (row, source_col(1, 0, 0)), (row, source_col(3, 0, 0))
    yh, sib = (row, source_col(0, 1, 0)), (row, source_col(0, 0, 1))
    neighbours = (xp, xm, yl, zp, zm, yh, sib)

    def rows_w(r, h):
        return pl.ds(pl.multiple_of(r * 128 + h * PIECE, PIECE), PIECE)

    def rows_a(s):
        return pl.ds(pl.multiple_of(s * PIECE, PIECE), PIECE)

    counts = [0, 0, 0]

    def copy_w(k, r, h, target, own=False):
        return pltpu.make_async_remote_copy(
            src_ref=w_in.at[k, pl.ds(h * PIECE, PIECE)] if own else W.at[k, rows_w(r, h)],
            dst_ref=W.at[k, rows_w(r, h)],
            send_sem=send_sem.at[k],
            recv_sem=recv_w.at[k, 2 * r + h],
            device_id=target,
            device_id_type=MESH,
        )

    def copy_a(k, i, s, target):
        return pltpu.make_async_remote_copy(
            src_ref=A.at[k, i, rows_a(s)],
            dst_ref=A.at[k, i, rows_a(s)],
            send_sem=send_sem.at[k],
            recv_sem=recv_a.at[k, i, s],
            device_id=target,
            device_id_type=MESH,
        )

    def send_w(k, r, h, *targets, own=False):
        for target in targets:
            copy_w(k, r, h, target, own).start()
            counts[k] += 1

    def send_a(k, i, s, *targets):
        for target in targets:
            copy_a(k, i, s, target).start()
            counts[k] += 1

    def wait_w(k, r, h):
        copy_w(k, r, h, yl).wait_recv()

    def wait_a(k, i, s):
        copy_a(k, i, s, sib).wait_recv()

    own_w, own_a = source_row(0, 0), source_col(0, 0, 0)

    def split(source, slot, first, count):
        def one(step, _):
            rows = pl.ds(pl.multiple_of(first + step * 64, 64), 64)
            high, low = parts(source[rows])
            SH[slot, rows] = high
            SL[slot, rows] = low
            return 0

        lax.fori_loop(0, count // 64, one, 0)

    def product(k, slot, group, depth_at, depth):
        rows = pl.ds(pl.multiple_of(group * 128, 128), 128)
        if depth == 1024:
            inner = slice(None)
        else:
            inner = pl.ds(pl.multiple_of(depth_at, depth), depth)
        a = A[k, :, rows, inner].reshape(256, depth)
        value = dot3(a, SH[slot, inner], SL[slot, inner])
        return rows, value.reshape(2, 128, 1024)

    def update(k, dz, dy, depth_at=0, depth=1024):
        group = ((z + dz) % 4) * 2 + (yhi + dy) % 2
        rows, value = product(k, k, group, depth_at, depth)
        before = parts_done[dz, dy]
        parts_done[dz, dy] = before + depth // 512
        if before == 0:
            C[:, rows] = value
        elif parts_done[dz, dy] < 6:
            C[:, rows] += value
        else:
            sums = jnp.concatenate([EA[rows]] * 8, axis=1) + EB[0:1, :]
            level_j = EI[2:3, 0:1]
            for i in (0, 1):
                denominator = (sums - EI[i : i + 1, 0:1]) - level_j
                C[i, rows] = (C[i, rows] + value[i]) / denominator

    chunk = 256
    loads = [
        pltpu.make_async_copy(
            dressing.at[pl.ds(at, chunk)], C.at[0, pl.ds(at, chunk)], local_sem.at[at // chunk]
        )
        for at in range(0, 1024, chunk)
    ]
    amp_loads = [
        pltpu.make_async_copy(amp.at[:, k], A.at[k, :, rows_a(own_a)], local_sem.at[4 + k])
        for k in range(3)
    ]
    w_load = pltpu.make_async_copy(
        w_in, W.at[:, pl.ds(pl.multiple_of(own_w * 128, 128), 128)], local_sem.at[7]
    )
    for load in (*loads, *amp_loads, w_load):
        load.start()
    barrier = pltpu.get_barrier_semaphore()
    for target in neighbours:
        pl.semaphore_signal(barrier, inc=1, device_id=target, device_id_type=MESH)
    pl.semaphore_wait(barrier, len(neighbours))

    def split_dressing():
        for number, load in enumerate(loads):
            load.wait()
            split(C.at[0], 2, number * chunk, chunk)

    def dress(k):
        amp_loads[k].wait()
        dressed = dot3(A[k, :, rows_a(own_a)].reshape(128, 1024), SH[2], SL[2])
        A[k, :, rows_a(own_a)] = dressed.reshape(2, PIECE, 1024)


    def energies():
        table = virtual_energy[...]
        lanes = lax.broadcasted_iota(jnp.int32, (128, 1024), 1)
        for at in range(0, 1024, 128):
            index = column(virtual_rows[:, at : at + 128])
            index = jnp.concatenate([index] * 8, axis=1)
            found = jnp.sum(jnp.where(index == lanes, table, 0.0), axis=1, keepdims=True)
            EA[at : at + 128] = jnp.broadcast_to(found, (128, 128))
            index = column(virtual_columns[:, at : at + 128])
            index = jnp.concatenate([index] * 8, axis=1)
            found = jnp.sum(jnp.where(index == lanes, table, 0.0), axis=1, keepdims=True)
            found = jnp.transpose(jnp.broadcast_to(found, (128, 128)))
            EB[:, at : at + 128] = found[:8]
        places = lax.broadcasted_iota(jnp.int32, (1, 128), 1)
        levels = (occupied_rows[0], occupied_rows[1], occupied_columns[0])
        for number, place in enumerate(levels):
            level = jnp.sum(
                jnp.where(places == place, occupied_energy[...], 0.0), axis=1, keepdims=True
            )
            EI[number : number + 1] = jnp.broadcast_to(level, (1, 128))

    links = {XP: xp, XM: xm, ZP: zp, ZM: zm}
    parts_done = {(d, dy): 0 for d in range(4) for dy in (0, 1)}
    seen, w_loaded = set(), [False]
    for step, *rest in PLAN:
        if step == SEND:
            link, array, k, d, dy, h = rest
            if array == INT:
                send_w(k, source_row(d, dy), h, links.get(link, yl), own=(d, dy) == (0, 0))
            else:
                send_a(k, h, source_col(d, dy, 0), links.get(link, yh))
        elif step == WAIT:
            array, k, d, dy, h = rest
            if array == INT:
                wait_w(k, source_row(d, dy), h)
            else:
                wait_a(k, h, source_col(d, dy, 0))
                send_a(k, h, source_col(d, dy, 0), sib)
        elif step == DRESSING:
            split_dressing()
        elif step == DRESS:
            (k,) = rest
            dress(k)
            for i in (0, 1):
                send_a(k, i, own_a, sib)
        elif step == ENERGY:
            energies()
        elif step == SPLIT:
            k, dy = rest
            if not w_loaded[0]:
                w_load.wait()
                w_loaded[0] = True
            split(W.at[k], k, ((ylo + dy) % 2) * 512, 512)
        else:
            k, dz, dy, *half = rest
            if (k, dz, dy) not in seen:
                seen.add((k, dz, dy))
                for i in (0, 1):
                    wait_a(k, i, source_col(dz, dy, 1))
            if half:
                update(k, dz, dy, ((ylo + half[0]) % 2) * 512, 512)
            else:
                update(k, dz, dy)

    for k in range(3):
        share = A.at[0:2, :, pl.ds(0, counts[k] * PIECE // 4)]
        pltpu.make_async_remote_copy(
            src_ref=share,
            dst_ref=share,
            send_sem=send_sem.at[k],
            recv_sem=recv_a.at[0, 0, 0],
            device_id=sib,
            device_id_type=MESH,
        ).wait_send()


def on_device(
    amplitudes,
    dressing,
    integrals,
    occupied_energy,
    virtual_energy,
    occupied_rows,
    virtual_rows,
    occupied_columns,
    virtual_columns,
):
    anywhere = pl.BlockSpec(memory_space=pl.ANY)
    vmem = pl.BlockSpec(memory_space=pltpu.VMEM)
    smem = pl.BlockSpec(memory_space=pltpu.SMEM)
    residual = pl.pallas_call(
        kernel,
        out_shape=pltpu.VMEM((2, 1024, 1024), F32),
        in_specs=[anywhere, anywhere, anywhere, vmem, vmem, smem, vmem, smem, vmem],
        out_specs=vmem,
        scratch_shapes=[
            pltpu.VMEM((3, 2, 1024, 1024), F32),
            pltpu.VMEM((3, 1024, 1024), F32),
            pltpu.VMEM((3, 1024, 1024), BF16),
            pltpu.VMEM((3, 1024, 1024), BF16),
            pltpu.VMEM((1024, 128), F32),
            pltpu.VMEM((8, 1024), F32),
            pltpu.VMEM((8, 128), F32),
            pltpu.SemaphoreType.DMA((3,)),
            pltpu.SemaphoreType.DMA((3, 16)),
            pltpu.SemaphoreType.DMA((3, 2, 16)),
            pltpu.SemaphoreType.DMA((8,)),
            pltpu.SemaphoreType.DMA((8,)),
        ],
        compiler_params=pltpu.CompilerParams(
            collective_id=0, has_side_effects=True, vmem_limit_bytes=55 * 2**20
        ),
        cost_estimate=pl.CostEstimate(
            flops=42_000_000_000, bytes_accessed=20_000_000, transcendentals=0
        ),
    )(
        amplitudes,
        dressing,
        jnp.transpose(integrals, (1, 0, 2)),
        occupied_energy.reshape(1, -1),
        virtual_energy.reshape(1, -1),
        occupied_rows,
        virtual_rows.reshape(1, -1),
        occupied_columns,
        virtual_columns.reshape(1, -1),
    )
    return residual.reshape(2048, 1024)


def solution(mesh):
    return jax.shard_map(
        on_device,
        mesh=mesh,
        in_specs=(
            P("row", None, "col", None),
            P(),
            P("row", None, "col"),
            P(),
            P(),
            P("row"),
            P(),
            P("col"),
            P(),
        ),
        out_specs=P("row", "col"),
        check_vma=False,
    )
```

```python
import functools

import jax
import jax.numpy as jnp
from jax import lax
from jax.experimental import pallas as pl
from jax.experimental.pallas import tpu as pltpu
from jax.sharding import PartitionSpec as P

MESH = pl.DeviceIdType.MESH
BF16, F32 = jnp.bfloat16, jnp.float32
WIDTH = 512
PIECE = 64

SEND, WAIT, DRESSING, DRESS, ENERGY, SPLIT, FULL, HALF = range(8)
XP, XM, ZP, ZM, Y = range(5)
INT, AMP = range(2)
PLAN = (
    (SEND, XP, INT, 0, 0, 0, 0), (SEND, XP, INT, 0, 0, 0, 1), (SEND, XM, INT, 0, 0, 0, 1),
    (SEND, XM, INT, 0, 0, 0, 0), (SEND, Y, INT, 0, 0, 0, 0), (SEND, Y, INT, 0, 0, 0, 1),
    (SEND, Y, INT, 1, 0, 0, 0), (DRESSING,), (DRESS, 0), (SEND, XP, INT, 1, 0, 0, 0),
    (SEND, XM, INT, 1, 0, 0, 1), (SEND, ZP, AMP, 0, 0, 0, 0), (SEND, ZP, AMP, 0, 0, 0, 1),
    (SEND, ZM, AMP, 0, 0, 0, 1), (SEND, ZM, AMP, 0, 0, 0, 0), (SEND, Y, AMP, 0, 0, 0, 0), (DRESS, 1),
    (WAIT, INT, 0, 3, 0, 0), (WAIT, INT, 0, 1, 0, 1), (WAIT, INT, 0, 0, 1, 0), (DRESS, 2), (ENERGY,),
    (SEND, XP, INT, 0, 3, 0, 0), (SEND, XM, INT, 0, 1, 0, 1), (SEND, Y, AMP, 0, 0, 0, 1),
    (SEND, ZP, AMP, 1, 0, 0, 0), (SEND, ZM, AMP, 1, 0, 0, 1), (WAIT, INT, 0, 3, 0, 1),
    (WAIT, INT, 0, 1, 0, 0), (WAIT, INT, 0, 0, 1, 1), (WAIT, AMP, 0, 3, 0, 0), (WAIT, AMP, 0, 1, 0, 1),
    (SEND, XP, INT, 0, 0, 1, 0), (SEND, XM, INT, 0, 0, 1, 1), (SEND, Y, AMP, 1, 0, 0, 0),
    (SEND, ZP, AMP, 0, 3, 0, 0), (SEND, ZM, AMP, 0, 1, 0, 1), (WAIT, INT, 1, 3, 0, 0),
    (WAIT, INT, 1, 1, 0, 1), (WAIT, INT, 1, 0, 1, 0), (WAIT, AMP, 0, 3, 0, 1), (WAIT, AMP, 0, 1, 0, 0),
    (SEND, XP, INT, 0, 0, 1, 1), (SEND, XM, INT, 0, 0, 1, 0), (SEND, Y, INT, 1, 0, 0, 1),
    (SEND, ZP, AMP, 1, 0, 0, 1), (SEND, ZM, AMP, 1, 0, 0, 0), (WAIT, INT, 0, 2, 0, 0),
    (WAIT, INT, 0, 2, 0, 1), (WAIT, AMP, 0, 0, 1, 0), (SPLIT, 0, 0), (WAIT, AMP, 1, 3, 0, 0),
    (WAIT, AMP, 1, 1, 0, 1), (HALF, 0, 0, 0, 0), (HALF, 0, 1, 0, 0), (HALF, 0, 3, 0, 0),
    (SEND, XP, INT, 1, 0, 0, 1), (SEND, XM, INT, 1, 0, 0, 0), (SEND, Y, AMP, 1, 0, 0, 1),
    (SEND, ZP, AMP, 0, 0, 1, 0), (SEND, ZM, AMP, 0, 0, 1, 0), (WAIT, INT, 0, 3, 1, 0),
    (WAIT, INT, 0, 1, 1, 1), (WAIT, AMP, 0, 0, 1, 1), (WAIT, AMP, 0, 2, 0, 0), (WAIT, AMP, 0, 2, 0, 1),
    (HALF, 0, 0, 1, 0), (HALF, 0, 2, 0, 0), (SEND, XP, INT, 0, 3, 1, 0), (SEND, XM, INT, 0, 1, 1, 1),
    (SEND, Y, INT, 2, 0, 0, 0), (SEND, ZP, AMP, 0, 0, 1, 1), (SEND, ZM, AMP, 0, 0, 1, 1),
    (WAIT, INT, 0, 3, 1, 1), (WAIT, INT, 0, 1, 1, 0), (WAIT, AMP, 1, 0, 1, 0), (WAIT, AMP, 1, 3, 0, 1),
    (WAIT, AMP, 1, 1, 0, 0), (SEND, XP, INT, 1, 3, 0, 0), (SEND, XM, INT, 1, 1, 0, 1),
    (SEND, Y, AMP, 2, 0, 0, 0), (SEND, ZP, AMP, 1, 3, 0, 0), (SEND, ZM, AMP, 1, 1, 0, 1),
    (WAIT, INT, 1, 3, 0, 1), (WAIT, INT, 1, 1, 0, 0), (WAIT, INT, 1, 0, 1, 1), (WAIT, AMP, 0, 3, 1, 0),
    (WAIT, AMP, 0, 1, 1, 0), (SEND, XP, INT, 1, 0, 1, 0), (SEND, XM, INT, 1, 0, 1, 1),
    (SEND, Y, INT, 2, 0, 0, 1), (SEND, ZP, AMP, 0, 3, 1, 0), (SEND, ZM, AMP, 1, 0, 1, 0),
    (WAIT, INT, 0, 2, 1, 0), (WAIT, INT, 0, 2, 1, 1), (WAIT, AMP, 1, 0, 1, 1), (SPLIT, 0, 1),
    (WAIT, AMP, 0, 3, 1, 1), (WAIT, AMP, 0, 1, 1, 1), (HALF, 0, 0, 0, 1), (HALF, 0, 0, 1, 1), (FULL, 0, 1, 1),
    (SEND, XP, INT, 1, 0, 1, 1), (SEND, XM, INT, 1, 0, 1, 0), (SEND, Y, AMP, 2, 0, 0, 1), (FULL, 0, 3, 1),
    (WAIT, INT, 1, 2, 0, 0), (WAIT, INT, 1, 2, 0, 1), (WAIT, INT, 2, 0, 1, 0), (WAIT, AMP, 1, 2, 0, 0),
    (WAIT, AMP, 1, 2, 0, 1), (SEND, ZP, AMP, 1, 0, 1, 0), (SEND, ZM, AMP, 0, 1, 1, 1), (HALF, 0, 1, 0, 1),
    (HALF, 0, 2, 0, 1), (HALF, 0, 3, 0, 1), (SEND, XP, INT, 2, 0, 0, 0), (SEND, XM, INT, 2, 0, 0, 1),
    (SEND, Y, INT, 1, 2, 0, 0), (SPLIT, 1, 0), (WAIT, INT, 1, 3, 1, 0), (WAIT, INT, 1, 1, 1, 1),
    (WAIT, AMP, 2, 0, 1, 0), (SEND, ZP, AMP, 1, 0, 1, 1), (SEND, ZM, AMP, 1, 0, 1, 1), (HALF, 1, 0, 0, 0),
    (WAIT, AMP, 0, 2, 1, 0), (WAIT, AMP, 1, 1, 1, 0), (HALF, 1, 0, 1, 0), (HALF, 1, 1, 0, 0),
    (HALF, 1, 2, 0, 0), (SEND, XP, INT, 2, 0, 0, 1), (SEND, XM, INT, 2, 0, 0, 0), (SEND, Y, INT, 1, 2, 0, 1),
    (HALF, 1, 3, 0, 0), (WAIT, INT, 1, 3, 1, 1), (WAIT, INT, 1, 1, 1, 0), (WAIT, INT, 2, 0, 1, 1),
    (SEND, ZP, AMP, 2, 0, 0, 0), (SEND, ZM, AMP, 2, 0, 0, 1), (WAIT, AMP, 1, 3, 1, 0),
    (WAIT, AMP, 0, 2, 1, 1), (FULL, 0, 2, 1), (SEND, XP, INT, 2, 0, 1, 0), (SEND, XM, INT, 2, 0, 1, 1),
    (SEND, Y, AMP, 1, 2, 0, 0), (SEND, ZP, AMP, 2, 0, 0, 1), (SEND, ZM, AMP, 2, 0, 0, 0),
    (WAIT, INT, 2, 3, 0, 0), (WAIT, INT, 2, 1, 0, 1), (WAIT, AMP, 2, 0, 1, 1), (WAIT, AMP, 1, 3, 1, 1),
    (WAIT, AMP, 1, 1, 1, 1), (HALF, 1, 3, 1, 0), (HALF, 1, 1, 1, 0), (SEND, XP, INT, 2, 3, 0, 0),
    (SEND, XM, INT, 2, 1, 0, 1), (SEND, Y, AMP, 1, 2, 0, 1), (SEND, ZP, AMP, 2, 0, 1, 0),
    (SEND, ZM, AMP, 2, 0, 1, 1), (WAIT, INT, 2, 3, 0, 1), (WAIT, INT, 2, 1, 0, 0), (WAIT, INT, 1, 2, 1, 0),
    (WAIT, AMP, 2, 3, 0, 0), (WAIT, AMP, 2, 1, 0, 1), (SEND, XP, INT, 2, 0, 1, 1),
    (SEND, XM, INT, 2, 0, 1, 0), (SEND, ZP, AMP, 2, 3, 0, 0), (SEND, ZM, AMP, 2, 1, 0, 1),
    (WAIT, INT, 2, 3, 1, 0), (WAIT, INT, 2, 1, 1, 1), (WAIT, INT, 1, 2, 1, 1), (SPLIT, 1, 1),
    (WAIT, AMP, 2, 3, 0, 1), (WAIT, AMP, 2, 1, 0, 0), (HALF, 1, 0, 0, 1), (HALF, 1, 0, 1, 1),
    (HALF, 1, 1, 0, 1), (HALF, 1, 1, 1, 1), (SEND, XP, INT, 2, 3, 1, 0), (SEND, XM, INT, 2, 1, 1, 1),
    (SEND, ZP, AMP, 2, 0, 1, 1), (SEND, ZM, AMP, 2, 0, 1, 0), (HALF, 1, 2, 0, 1), (WAIT, INT, 2, 2, 0, 0),
    (WAIT, INT, 2, 2, 0, 1), (WAIT, AMP, 1, 2, 1, 0), (WAIT, AMP, 2, 3, 1, 0), (WAIT, AMP, 2, 1, 1, 1),
    (HALF, 1, 3, 0, 1), (HALF, 1, 3, 1, 1), (SPLIT, 2, 0), (HALF, 2, 0, 0, 0), (SEND, ZP, AMP, 2, 3, 1, 0),
    (SEND, ZM, AMP, 2, 1, 1, 1), (HALF, 2, 0, 1, 0), (WAIT, INT, 2, 3, 1, 1), (WAIT, INT, 2, 1, 1, 0),
    (WAIT, AMP, 1, 2, 1, 1), (WAIT, AMP, 2, 2, 0, 0), (WAIT, AMP, 2, 2, 0, 1), (HALF, 2, 1, 0, 0),
    (HALF, 2, 3, 0, 0), (FULL, 1, 2, 1), (HALF, 2, 2, 0, 0), (WAIT, INT, 2, 2, 1, 0), (WAIT, INT, 2, 2, 1, 1),
    (SPLIT, 2, 1), (WAIT, AMP, 2, 3, 1, 1), (WAIT, AMP, 2, 1, 1, 0), (HALF, 2, 0, 0, 1), (HALF, 2, 0, 1, 1),
    (FULL, 2, 1, 1), (FULL, 2, 3, 1), (WAIT, AMP, 2, 2, 1, 0), (WAIT, AMP, 2, 2, 1, 1), (HALF, 2, 1, 0, 1),
    (HALF, 2, 2, 0, 1), (FULL, 2, 2, 1), (HALF, 2, 3, 0, 1),
)


def parts(values):
    high = values.astype(BF16)
    return high, (values - high.astype(F32)).astype(BF16)


def dot(a, b):
    return jnp.dot(a, b, preferred_element_type=F32)


def dot3(a, b_high, b_low):
    a_high, a_low = parts(a)
    return dot(a_high, b_high) + dot(a_high, b_low) + dot(a_low, b_high)


def column(row):
    tiles = [
        jnp.transpose(jnp.broadcast_to(row[:, at : at + 128], (128, 128)))
        for at in range(0, row.shape[1], 128)
    ]
    return jnp.concatenate(tiles, axis=0)


def kernel(
    amp,
    dressing,
    w_in,
    occupied_energy,
    virtual_energy,
    occupied_rows,
    virtual_rows,
    occupied_columns,
    virtual_columns,
    C,
    A,
    W,
    SH,
    SL,
    EA,
    EB,
    EI,
    send_sem,
    recv_w,
    recv_a,
    local_sem,
    out_sem,
):
    row, col = lax.axis_index("row"), lax.axis_index("col")
    x, ylo = row % 4, row // 4
    z, yhi, core = col // 4, (col // 2) % 2, col % 2

    def source_row(dx, dy):
        return ((ylo + dy) % 2) * 4 + (x + dx) % 4

    def source_col(dz, dy, dcore):
        return ((z + dz) % 4) * 4 + ((yhi + dy) % 2) * 2 + (core + dcore) % 2

    xp, xm, yl = (source_row(1, 0), col), (source_row(3, 0), col), (source_row(0, 1), col)
    zp, zm = (row, source_col(1, 0, 0)), (row, source_col(3, 0, 0))
    yh, sib = (row, source_col(0, 1, 0)), (row, source_col(0, 0, 1))
    neighbours = (xp, xm, yl, zp, zm, yh, sib)

    def rows_w(r, h):
        return pl.ds(pl.multiple_of(r * 128 + h * PIECE, PIECE), PIECE)

    def rows_a(s):
        return pl.ds(pl.multiple_of(s * PIECE, PIECE), PIECE)

    counts = [0, 0, 0]

    def copy_w(k, r, h, target, own=False):
        return pltpu.make_async_remote_copy(
            src_ref=w_in.at[k, pl.ds(h * PIECE, PIECE)] if own else W.at[k, rows_w(r, h)],
            dst_ref=W.at[k, rows_w(r, h)],
            send_sem=send_sem.at[k],
            recv_sem=recv_w.at[k, 2 * r + h],
            device_id=target,
            device_id_type=MESH,
        )

    def copy_a(k, i, s, target):
        return pltpu.make_async_remote_copy(
            src_ref=A.at[k, i, rows_a(s)],
            dst_ref=A.at[k, i, rows_a(s)],
            send_sem=send_sem.at[k],
            recv_sem=recv_a.at[k, i, s],
            device_id=target,
            device_id_type=MESH,
        )

    def send_w(k, r, h, *targets, own=False):
        for target in targets:
            copy_w(k, r, h, target, own).start()
            counts[k] += 1

    def send_a(k, i, s, *targets):
        for target in targets:
            copy_a(k, i, s, target).start()
            counts[k] += 1

    def wait_w(k, r, h):
        copy_w(k, r, h, yl).wait_recv()

    def wait_a(k, i, s):
        copy_a(k, i, s, sib).wait_recv()

    own_w, own_a = source_row(0, 0), source_col(0, 0, 0)

    def split(source, slot, first, count):
        def one(step, _):
            rows = pl.ds(pl.multiple_of(first + step * 64, 64), 64)
            high, low = parts(source[rows])
            SH[slot, rows] = high
            SL[slot, rows] = low
            return 0

        lax.fori_loop(0, count // 64, one, 0)

    def update(k, dz, dy, depth_at=0, depth=1024):
        group = ((z + dz) % 4) * 2 + (yhi + dy) % 2
        rows = pl.ds(pl.multiple_of(group * 128, 128), 128)
        if depth == 1024:
            inner = slice(None)
        else:
            inner = pl.ds(pl.multiple_of(depth_at, depth), depth)
        before = parts_done[dz, dy]
        parts_done[dz, dy] = before + depth // 512
        last = parts_done[dz, dy] == 6

        def one(step, _):
            columns = pl.ds(pl.multiple_of(step * WIDTH, WIDTH), WIDTH)
            a = A[k, :, rows, inner].reshape(256, depth)
            value = dot3(a, SH[k, inner, columns], SL[k, inner, columns])
            value = value.reshape(2, 128, WIDTH)
            if before == 0:
                C[:, rows, columns] = value
            elif not last:
                C[:, rows, columns] += value
            else:
                sums = jnp.concatenate([EA[rows]] * (WIDTH // 128), axis=1) + EB[0:1, columns]
                level_j = EI[2:3, 0:1]
                for i in (0, 1):
                    denominator = (sums - EI[i : i + 1, 0:1]) - level_j
                    C[i, rows, columns] = (C[i, rows, columns] + value[i]) / denominator
            return 0

        lax.fori_loop(0, 1024 // WIDTH, one, 0)

    chunk = 256
    loads = [
        pltpu.make_async_copy(
            dressing.at[pl.ds(at, chunk)], C.at[0, pl.ds(at, chunk)], local_sem.at[at // chunk]
        )
        for at in range(0, 1024, chunk)
    ]
    amp_loads = [
        pltpu.make_async_copy(amp.at[:, k], A.at[k, :, rows_a(own_a)], local_sem.at[4 + k])
        for k in range(3)
    ]
    w_load = pltpu.make_async_copy(
        w_in, W.at[:, pl.ds(pl.multiple_of(own_w * 128, 128), 128)], local_sem.at[7]
    )
    for load in (*loads, *amp_loads, w_load):
        load.start()
    barrier = pltpu.get_barrier_semaphore()
    for target in neighbours:
        pl.semaphore_signal(barrier, inc=1, device_id=target, device_id_type=MESH)
    pl.semaphore_wait(barrier, len(neighbours))

    def split_dressing():
        for number, load in enumerate(loads):
            load.wait()
            split(C.at[0], 2, number * chunk, chunk)

    def dress(k):
        amp_loads[k].wait()
        dressed = dot3(A[k, :, rows_a(own_a)].reshape(128, 1024), SH[2], SL[2])
        A[k, :, rows_a(own_a)] = dressed.reshape(2, PIECE, 1024)


    def energies():
        table = virtual_energy[...]
        lanes = lax.broadcasted_iota(jnp.int32, (128, 1024), 1)
        for at in range(0, 1024, 128):
            index = column(virtual_rows[:, at : at + 128])
            index = jnp.concatenate([index] * 8, axis=1)
            found = jnp.sum(jnp.where(index == lanes, table, 0.0), axis=1, keepdims=True)
            EA[at : at + 128] = jnp.broadcast_to(found, (128, 128))
            index = column(virtual_columns[:, at : at + 128])
            index = jnp.concatenate([index] * 8, axis=1)
            found = jnp.sum(jnp.where(index == lanes, table, 0.0), axis=1, keepdims=True)
            found = jnp.transpose(jnp.broadcast_to(found, (128, 128)))
            EB[:, at : at + 128] = found[:8]
        places = lax.broadcasted_iota(jnp.int32, (1, 128), 1)
        levels = (occupied_rows[0], occupied_rows[1], occupied_columns[0])
        for number, place in enumerate(levels):
            level = jnp.sum(
                jnp.where(places == place, occupied_energy[...], 0.0), axis=1, keepdims=True
            )
            EI[number : number + 1] = jnp.broadcast_to(level, (1, 128))

    links = {XP: xp, XM: xm, ZP: zp, ZM: zm}
    parts_done = {(d, dy): 0 for d in range(4) for dy in (0, 1)}
    seen, w_loaded = set(), [False]
    for step, *rest in PLAN:
        if step == SEND:
            link, array, k, d, dy, h = rest
            if array == INT:
                send_w(k, source_row(d, dy), h, links.get(link, yl), own=(d, dy) == (0, 0))
            else:
                send_a(k, h, source_col(d, dy, 0), links.get(link, yh))
        elif step == WAIT:
            array, k, d, dy, h = rest
            if array == INT:
                wait_w(k, source_row(d, dy), h)
            else:
                wait_a(k, h, source_col(d, dy, 0))
                send_a(k, h, source_col(d, dy, 0), sib)
        elif step == DRESSING:
            split_dressing()
        elif step == DRESS:
            (k,) = rest
            dress(k)
            for i in (0, 1):
                send_a(k, i, own_a, sib)
        elif step == ENERGY:
            energies()
        elif step == SPLIT:
            k, dy = rest
            if not w_loaded[0]:
                w_load.wait()
                w_loaded[0] = True
            split(W.at[k], k, ((ylo + dy) % 2) * 512, 512)
        else:
            k, dz, dy, *half = rest
            if (k, dz, dy) not in seen:
                seen.add((k, dz, dy))
                for i in (0, 1):
                    wait_a(k, i, source_col(dz, dy, 1))
            if half:
                update(k, dz, dy, ((ylo + half[0]) % 2) * 512, 512)
            else:
                update(k, dz, dy)

    for k in range(3):
        share = A.at[0:2, :, pl.ds(0, counts[k] * PIECE // 4)]
        pltpu.make_async_remote_copy(
            src_ref=share,
            dst_ref=share,
            send_sem=send_sem.at[k],
            recv_sem=recv_a.at[0, 0, 0],
            device_id=sib,
            device_id_type=MESH,
        ).wait_send()


def on_device(
    amplitudes,
    dressing,
    integrals,
    occupied_energy,
    virtual_energy,
    occupied_rows,
    virtual_rows,
    occupied_columns,
    virtual_columns,
):
    anywhere = pl.BlockSpec(memory_space=pl.ANY)
    vmem = pl.BlockSpec(memory_space=pltpu.VMEM)
    smem = pl.BlockSpec(memory_space=pltpu.SMEM)
    residual = pl.pallas_call(
        kernel,
        out_shape=pltpu.VMEM((2, 1024, 1024), F32),
        in_specs=[anywhere, anywhere, anywhere, vmem, vmem, smem, vmem, smem, vmem],
        out_specs=vmem,
        scratch_shapes=[
            pltpu.VMEM((3, 2, 1024, 1024), F32),
            pltpu.VMEM((3, 1024, 1024), F32),
            pltpu.VMEM((3, 1024, 1024), BF16),
            pltpu.VMEM((3, 1024, 1024), BF16),
            pltpu.VMEM((1024, 128), F32),
            pltpu.VMEM((8, 1024), F32),
            pltpu.VMEM((8, 128), F32),
            pltpu.SemaphoreType.DMA((3,)),
            pltpu.SemaphoreType.DMA((3, 16)),
            pltpu.SemaphoreType.DMA((3, 2, 16)),
            pltpu.SemaphoreType.DMA((8,)),
            pltpu.SemaphoreType.DMA((8,)),
        ],
        compiler_params=pltpu.CompilerParams(
            collective_id=0, has_side_effects=True, vmem_limit_bytes=55 * 2**20
        ),
        cost_estimate=pl.CostEstimate(
            flops=42_000_000_000, bytes_accessed=20_000_000, transcendentals=0
        ),
    )(
        amplitudes,
        dressing,
        jnp.transpose(integrals, (1, 0, 2)),
        occupied_energy.reshape(1, -1),
        virtual_energy.reshape(1, -1),
        occupied_rows,
        virtual_rows.reshape(1, -1),
        occupied_columns,
        virtual_columns.reshape(1, -1),
    )
    return residual.reshape(2048, 1024)


def solution(mesh):
    return jax.shard_map(
        on_device,
        mesh=mesh,
        in_specs=(
            P("row", None, "col", None),
            P(),
            P("row", None, "col"),
            P(),
            P(),
            P("row"),
            P(),
            P("col"),
            P(),
        ),
        out_specs=P("row", "col"),
        check_vma=False,
    )
```

```python
import functools

import jax
import jax.numpy as jnp
from jax import lax
from jax.experimental import pallas as pl
from jax.experimental.pallas import tpu as pltpu
from jax.sharding import PartitionSpec as P

MESH = pl.DeviceIdType.MESH
BF16, F32 = jnp.bfloat16, jnp.float32
WIDTHS = (512, 512, 1024)
PIECE = 64

SEND, WAIT, DRESSING, DRESS, ENERGY, SPLIT, FULL, HALF = range(8)
XP, XM, ZP, ZM, Y = range(5)
INT, AMP = range(2)
PLAN = (
    (SEND, XP, INT, 0, 0, 0, 0), (SEND, XP, INT, 0, 0, 0, 1), (SEND, XM, INT, 0, 0, 0, 1),
    (SEND, XM, INT, 0, 0, 0, 0), (SEND, Y, INT, 0, 0, 0, 0), (SEND, Y, INT, 0, 0, 0, 1),
    (SEND, Y, INT, 1, 0, 0, 0), (DRESSING,), (DRESS, 0), (SEND, XP, INT, 1, 0, 0, 0),
    (SEND, XM, INT, 1, 0, 0, 1), (SEND, ZP, AMP, 0, 0, 0, 0), (SEND, ZP, AMP, 0, 0, 0, 1),
    (SEND, ZM, AMP, 0, 0, 0, 1), (SEND, ZM, AMP, 0, 0, 0, 0), (SEND, Y, AMP, 0, 0, 0, 0), (DRESS, 1),
    (WAIT, INT, 0, 3, 0, 0), (WAIT, INT, 0, 1, 0, 1), (WAIT, INT, 0, 0, 1, 0), (DRESS, 2), (ENERGY,),
    (SEND, XP, INT, 0, 3, 0, 0), (SEND, XM, INT, 0, 1, 0, 1), (SEND, Y, AMP, 0, 0, 0, 1),
    (SEND, ZP, AMP, 1, 0, 0, 0), (SEND, ZM, AMP, 1, 0, 0, 1), (WAIT, INT, 0, 3, 0, 1),
    (WAIT, INT, 0, 1, 0, 0), (WAIT, INT, 0, 0, 1, 1), (WAIT, AMP, 0, 3, 0, 0), (WAIT, AMP, 0, 1, 0, 1),
    (SEND, XP, INT, 0, 0, 1, 0), (SEND, XM, INT, 0, 0, 1, 1), (SEND, Y, AMP, 1, 0, 0, 0),
    (SEND, ZP, AMP, 0, 3, 0, 0), (SEND, ZM, AMP, 0, 1, 0, 1), (WAIT, INT, 1, 3, 0, 0),
    (WAIT, INT, 1, 1, 0, 1), (WAIT, INT, 1, 0, 1, 0), (WAIT, AMP, 0, 3, 0, 1), (WAIT, AMP, 0, 1, 0, 0),
    (SEND, XP, INT, 0, 0, 1, 1), (SEND, XM, INT, 0, 0, 1, 0), (SEND, Y, INT, 1, 0, 0, 1),
    (SEND, ZP, AMP, 1, 0, 0, 1), (SEND, ZM, AMP, 1, 0, 0, 0), (WAIT, INT, 0, 2, 0, 0),
    (WAIT, INT, 0, 2, 0, 1), (WAIT, AMP, 0, 0, 1, 0), (SPLIT, 0, 0), (WAIT, AMP, 1, 3, 0, 0),
    (WAIT, AMP, 1, 1, 0, 1), (HALF, 0, 0, 0, 0), (HALF, 0, 1, 0, 0), (HALF, 0, 3, 0, 0),
    (SEND, XP, INT, 1, 0, 0, 1), (SEND, XM, INT, 1, 0, 0, 0), (SEND, Y, AMP, 1, 0, 0, 1),
    (SEND, ZP, AMP, 0, 0, 1, 0), (SEND, ZM, AMP, 0, 0, 1, 0), (WAIT, INT, 0, 3, 1, 0),
    (WAIT, INT, 0, 1, 1, 1), (WAIT, AMP, 0, 0, 1, 1), (WAIT, AMP, 0, 2, 0, 0), (WAIT, AMP, 0, 2, 0, 1),
    (HALF, 0, 0, 1, 0), (HALF, 0, 2, 0, 0), (SEND, XP, INT, 0, 3, 1, 0), (SEND, XM, INT, 0, 1, 1, 1),
    (SEND, Y, INT, 2, 0, 0, 0), (SEND, ZP, AMP, 0, 0, 1, 1), (SEND, ZM, AMP, 0, 0, 1, 1),
    (WAIT, INT, 0, 3, 1, 1), (WAIT, INT, 0, 1, 1, 0), (WAIT, AMP, 1, 0, 1, 0), (WAIT, AMP, 1, 3, 0, 1),
    (WAIT, AMP, 1, 1, 0, 0), (SEND, XP, INT, 1, 3, 0, 0), (SEND, XM, INT, 1, 1, 0, 1),
    (SEND, Y, AMP, 2, 0, 0, 0), (SEND, ZP, AMP, 1, 3, 0, 0), (SEND, ZM, AMP, 1, 1, 0, 1),
    (WAIT, INT, 1, 3, 0, 1), (WAIT, INT, 1, 1, 0, 0), (WAIT, INT, 1, 0, 1, 1), (WAIT, AMP, 0, 3, 1, 0),
    (WAIT, AMP, 0, 1, 1, 0), (SEND, XP, INT, 1, 0, 1, 0), (SEND, XM, INT, 1, 0, 1, 1),
    (SEND, Y, INT, 2, 0, 0, 1), (SEND, ZP, AMP, 0, 3, 1, 0), (SEND, ZM, AMP, 1, 0, 1, 0),
    (WAIT, INT, 0, 2, 1, 0), (WAIT, INT, 0, 2, 1, 1), (WAIT, AMP, 1, 0, 1, 1), (SPLIT, 0, 1),
    (WAIT, AMP, 0, 3, 1, 1), (WAIT, AMP, 0, 1, 1, 1), (HALF, 0, 0, 0, 1), (HALF, 0, 0, 1, 1), (FULL, 0, 1, 1),
    (SEND, XP, INT, 1, 0, 1, 1), (SEND, XM, INT, 1, 0, 1, 0), (SEND, Y, AMP, 2, 0, 0, 1), (FULL, 0, 3, 1),
    (WAIT, INT, 1, 2, 0, 0), (WAIT, INT, 1, 2, 0, 1), (WAIT, INT, 2, 0, 1, 0), (WAIT, AMP, 1, 2, 0, 0),
    (WAIT, AMP, 1, 2, 0, 1), (SEND, ZP, AMP, 1, 0, 1, 0), (SEND, ZM, AMP, 0, 1, 1, 1), (HALF, 0, 1, 0, 1),
    (HALF, 0, 2, 0, 1), (HALF, 0, 3, 0, 1), (SEND, XP, INT, 2, 0, 0, 0), (SEND, XM, INT, 2, 0, 0, 1),
    (SEND, Y, INT, 1, 2, 0, 0), (SPLIT, 1, 0), (WAIT, INT, 1, 3, 1, 0), (WAIT, INT, 1, 1, 1, 1),
    (WAIT, AMP, 2, 0, 1, 0), (SEND, ZP, AMP, 1, 0, 1, 1), (SEND, ZM, AMP, 1, 0, 1, 1), (HALF, 1, 0, 0, 0),
    (WAIT, AMP, 0, 2, 1, 0), (WAIT, AMP, 1, 1, 1, 0), (HALF, 1, 0, 1, 0), (HALF, 1, 1, 0, 0),
    (HALF, 1, 2, 0, 0), (SEND, XP, INT, 2, 0, 0, 1), (SEND, XM, INT, 2, 0, 0, 0), (SEND, Y, INT, 1, 2, 0, 1),
    (HALF, 1, 3, 0, 0), (WAIT, INT, 1, 3, 1, 1), (WAIT, INT, 1, 1, 1, 0), (WAIT, INT, 2, 0, 1, 1),
    (SEND, ZP, AMP, 2, 0, 0, 0), (SEND, ZM, AMP, 2, 0, 0, 1), (WAIT, AMP, 1, 3, 1, 0),
    (WAIT, AMP, 0, 2, 1, 1), (FULL, 0, 2, 1), (SEND, XP, INT, 2, 0, 1, 0), (SEND, XM, INT, 2, 0, 1, 1),
    (SEND, Y, AMP, 1, 2, 0, 0), (SEND, ZP, AMP, 2, 0, 0, 1), (SEND, ZM, AMP, 2, 0, 0, 0),
    (WAIT, INT, 2, 3, 0, 0), (WAIT, INT, 2, 1, 0, 1), (WAIT, AMP, 2, 0, 1, 1), (WAIT, AMP, 1, 3, 1, 1),
    (WAIT, AMP, 1, 1, 1, 1), (HALF, 1, 3, 1, 0), (HALF, 1, 1, 1, 0), (SEND, XP, INT, 2, 3, 0, 0),
    (SEND, XM, INT, 2, 1, 0, 1), (SEND, Y, AMP, 1, 2, 0, 1), (SEND, ZP, AMP, 2, 0, 1, 0),
    (SEND, ZM, AMP, 2, 0, 1, 1), (WAIT, INT, 2, 3, 0, 1), (WAIT, INT, 2, 1, 0, 0), (WAIT, INT, 1, 2, 1, 0),
    (WAIT, AMP, 2, 3, 0, 0), (WAIT, AMP, 2, 1, 0, 1), (SEND, XP, INT, 2, 0, 1, 1),
    (SEND, XM, INT, 2, 0, 1, 0), (SEND, ZP, AMP, 2, 3, 0, 0), (SEND, ZM, AMP, 2, 1, 0, 1),
    (WAIT, INT, 2, 3, 1, 0), (WAIT, INT, 2, 1, 1, 1), (WAIT, INT, 1, 2, 1, 1), (SPLIT, 1, 1),
    (WAIT, AMP, 2, 3, 0, 1), (WAIT, AMP, 2, 1, 0, 0), (HALF, 1, 0, 0, 1), (HALF, 1, 0, 1, 1),
    (HALF, 1, 1, 0, 1), (HALF, 1, 1, 1, 1), (SEND, XP, INT, 2, 3, 1, 0), (SEND, XM, INT, 2, 1, 1, 1),
    (SEND, ZP, AMP, 2, 0, 1, 1), (SEND, ZM, AMP, 2, 0, 1, 0), (HALF, 1, 2, 0, 1), (WAIT, INT, 2, 2, 0, 0),
    (WAIT, INT, 2, 2, 0, 1), (WAIT, AMP, 1, 2, 1, 0), (WAIT, AMP, 2, 3, 1, 0), (WAIT, AMP, 2, 1, 1, 1),
    (HALF, 1, 3, 0, 1), (HALF, 1, 3, 1, 1), (SPLIT, 2, 0), (HALF, 2, 0, 0, 0), (SEND, ZP, AMP, 2, 3, 1, 0),
    (SEND, ZM, AMP, 2, 1, 1, 1), (HALF, 2, 0, 1, 0), (WAIT, INT, 2, 3, 1, 1), (WAIT, INT, 2, 1, 1, 0),
    (WAIT, AMP, 1, 2, 1, 1), (WAIT, AMP, 2, 2, 0, 0), (WAIT, AMP, 2, 2, 0, 1), (HALF, 2, 1, 0, 0),
    (HALF, 2, 3, 0, 0), (FULL, 1, 2, 1), (HALF, 2, 2, 0, 0), (WAIT, INT, 2, 2, 1, 0), (WAIT, INT, 2, 2, 1, 1),
    (SPLIT, 2, 1), (WAIT, AMP, 2, 3, 1, 1), (WAIT, AMP, 2, 1, 1, 0), (HALF, 2, 0, 0, 1), (HALF, 2, 0, 1, 1),
    (FULL, 2, 1, 1), (FULL, 2, 3, 1), (WAIT, AMP, 2, 2, 1, 0), (WAIT, AMP, 2, 2, 1, 1), (HALF, 2, 1, 0, 1),
    (HALF, 2, 2, 0, 1), (FULL, 2, 2, 1), (HALF, 2, 3, 0, 1),
)


def parts(values):
    high = values.astype(BF16)
    return high, (values - high.astype(F32)).astype(BF16)


def dot(a, b):
    return jnp.dot(a, b, preferred_element_type=F32)


def dot3(a, b_high, b_low):
    a_high, a_low = parts(a)
    return dot(a_high, b_high) + dot(a_high, b_low) + dot(a_low, b_high)


def column(row):
    tiles = [
        jnp.transpose(jnp.broadcast_to(row[:, at : at + 128], (128, 128)))
        for at in range(0, row.shape[1], 128)
    ]
    return jnp.concatenate(tiles, axis=0)


def kernel(
    amp,
    dressing,
    w_in,
    occupied_energy,
    virtual_energy,
    occupied_rows,
    virtual_rows,
    occupied_columns,
    virtual_columns,
    C,
    A,
    W,
    SH,
    SL,
    EA,
    EB,
    EI,
    send_sem,
    recv_w,
    recv_a,
    local_sem,
    out_sem,
):
    row, col = lax.axis_index("row"), lax.axis_index("col")
    x, ylo = row % 4, row // 4
    z, yhi, core = col // 4, (col // 2) % 2, col % 2

    def source_row(dx, dy):
        return ((ylo + dy) % 2) * 4 + (x + dx) % 4

    def source_col(dz, dy, dcore):
        return ((z + dz) % 4) * 4 + ((yhi + dy) % 2) * 2 + (core + dcore) % 2

    xp, xm, yl = (source_row(1, 0), col), (source_row(3, 0), col), (source_row(0, 1), col)
    zp, zm = (row, source_col(1, 0, 0)), (row, source_col(3, 0, 0))
    yh, sib = (row, source_col(0, 1, 0)), (row, source_col(0, 0, 1))
    neighbours = (xp, xm, yl, zp, zm, yh, sib)

    def rows_w(r, h):
        return pl.ds(pl.multiple_of(r * 128 + h * PIECE, PIECE), PIECE)

    def rows_a(s):
        return pl.ds(pl.multiple_of(s * PIECE, PIECE), PIECE)

    counts = [0, 0, 0]

    def copy_w(k, r, h, target, own=False):
        return pltpu.make_async_remote_copy(
            src_ref=w_in.at[k, pl.ds(h * PIECE, PIECE)] if own else W.at[k, rows_w(r, h)],
            dst_ref=W.at[k, rows_w(r, h)],
            send_sem=send_sem.at[k],
            recv_sem=recv_w.at[k, 2 * r + h],
            device_id=target,
            device_id_type=MESH,
        )

    def copy_a(k, i, s, target):
        return pltpu.make_async_remote_copy(
            src_ref=A.at[k, i, rows_a(s)],
            dst_ref=A.at[k, i, rows_a(s)],
            send_sem=send_sem.at[k],
            recv_sem=recv_a.at[k, i, s],
            device_id=target,
            device_id_type=MESH,
        )

    def send_w(k, r, h, *targets, own=False):
        for target in targets:
            copy_w(k, r, h, target, own).start()
            counts[k] += 1

    def send_a(k, i, s, *targets):
        for target in targets:
            copy_a(k, i, s, target).start()
            counts[k] += 1

    def wait_w(k, r, h):
        copy_w(k, r, h, yl).wait_recv()

    def wait_a(k, i, s):
        copy_a(k, i, s, sib).wait_recv()

    own_w, own_a = source_row(0, 0), source_col(0, 0, 0)

    def split(source, slot, first, count):
        def one(step, _):
            rows = pl.ds(pl.multiple_of(first + step * 64, 64), 64)
            high, low = parts(source[rows])
            SH[slot, rows] = high
            SL[slot, rows] = low
            return 0

        lax.fori_loop(0, count // 64, one, 0)

    def update(k, dz, dy, depth_at=0, depth=1024):
        group = ((z + dz) % 4) * 2 + (yhi + dy) % 2
        rows = pl.ds(pl.multiple_of(group * 128, 128), 128)
        if depth == 1024:
            inner = slice(None)
        else:
            inner = pl.ds(pl.multiple_of(depth_at, depth), depth)
        before = parts_done[dz, dy]
        parts_done[dz, dy] = before + depth // 512
        last = parts_done[dz, dy] == 6

        width = WIDTHS[k]

        def one(step, _):
            columns = slice(None) if width == 1024 else pl.ds(pl.multiple_of(step * width, width), width)
            a = A[k, :, rows, inner].reshape(256, depth)
            value = dot3(a, SH[k, inner, columns], SL[k, inner, columns])
            value = value.reshape(2, 128, width)
            if before == 0:
                C[:, rows, columns] = value
            elif not last:
                C[:, rows, columns] += value
            else:
                sums = jnp.concatenate([EA[rows]] * (width // 128), axis=1) + EB[0:1, columns]
                level_j = EI[2:3, 0:1]
                for i in (0, 1):
                    denominator = (sums - EI[i : i + 1, 0:1]) - level_j
                    C[i, rows, columns] = (C[i, rows, columns] + value[i]) / denominator
            return 0

        if width == 1024:
            one(0, 0)
        else:
            lax.fori_loop(0, 1024 // width, one, 0)

    chunk = 256
    loads = [
        pltpu.make_async_copy(
            dressing.at[pl.ds(at, chunk)], C.at[0, pl.ds(at, chunk)], local_sem.at[at // chunk]
        )
        for at in range(0, 1024, chunk)
    ]
    amp_loads = [
        pltpu.make_async_copy(amp.at[:, k], A.at[k, :, rows_a(own_a)], local_sem.at[4 + k])
        for k in range(3)
    ]
    w_load = pltpu.make_async_copy(
        w_in, W.at[:, pl.ds(pl.multiple_of(own_w * 128, 128), 128)], local_sem.at[7]
    )
    for load in (*loads, *amp_loads, w_load):
        load.start()
    barrier = pltpu.get_barrier_semaphore()
    for target in neighbours:
        pl.semaphore_signal(barrier, inc=1, device_id=target, device_id_type=MESH)
    pl.semaphore_wait(barrier, len(neighbours))

    def split_dressing():
        for number, load in enumerate(loads):
            load.wait()
            split(C.at[0], 2, number * chunk, chunk)

    def dress(k):
        amp_loads[k].wait()
        dressed = dot3(A[k, :, rows_a(own_a)].reshape(128, 1024), SH[2], SL[2])
        A[k, :, rows_a(own_a)] = dressed.reshape(2, PIECE, 1024)


    def energies():
        table = virtual_energy[...]
        lanes = lax.broadcasted_iota(jnp.int32, (128, 1024), 1)
        for at in range(0, 1024, 128):
            index = column(virtual_rows[:, at : at + 128])
            index = jnp.concatenate([index] * 8, axis=1)
            found = jnp.sum(jnp.where(index == lanes, table, 0.0), axis=1, keepdims=True)
            EA[at : at + 128] = jnp.broadcast_to(found, (128, 128))
            index = column(virtual_columns[:, at : at + 128])
            index = jnp.concatenate([index] * 8, axis=1)
            found = jnp.sum(jnp.where(index == lanes, table, 0.0), axis=1, keepdims=True)
            found = jnp.transpose(jnp.broadcast_to(found, (128, 128)))
            EB[:, at : at + 128] = found[:8]
        places = lax.broadcasted_iota(jnp.int32, (1, 128), 1)
        levels = (occupied_rows[0], occupied_rows[1], occupied_columns[0])
        for number, place in enumerate(levels):
            level = jnp.sum(
                jnp.where(places == place, occupied_energy[...], 0.0), axis=1, keepdims=True
            )
            EI[number : number + 1] = jnp.broadcast_to(level, (1, 128))

    links = {XP: xp, XM: xm, ZP: zp, ZM: zm}
    parts_done = {(d, dy): 0 for d in range(4) for dy in (0, 1)}
    seen, w_loaded = set(), [False]
    for step, *rest in PLAN:
        if step == SEND:
            link, array, k, d, dy, h = rest
            if array == INT:
                send_w(k, source_row(d, dy), h, links.get(link, yl), own=(d, dy) == (0, 0))
            else:
                send_a(k, h, source_col(d, dy, 0), links.get(link, yh))
        elif step == WAIT:
            array, k, d, dy, h = rest
            if array == INT:
                wait_w(k, source_row(d, dy), h)
            else:
                wait_a(k, h, source_col(d, dy, 0))
                send_a(k, h, source_col(d, dy, 0), sib)
        elif step == DRESSING:
            split_dressing()
        elif step == DRESS:
            (k,) = rest
            dress(k)
            for i in (0, 1):
                send_a(k, i, own_a, sib)
        elif step == ENERGY:
            energies()
        elif step == SPLIT:
            k, dy = rest
            if not w_loaded[0]:
                w_load.wait()
                w_loaded[0] = True
            split(W.at[k], k, ((ylo + dy) % 2) * 512, 512)
        else:
            k, dz, dy, *half = rest
            if (k, dz, dy) not in seen:
                seen.add((k, dz, dy))
                for i in (0, 1):
                    wait_a(k, i, source_col(dz, dy, 1))
            if half:
                update(k, dz, dy, ((ylo + half[0]) % 2) * 512, 512)
            else:
                update(k, dz, dy)

    for k in range(3):
        share = A.at[0:2, :, pl.ds(0, counts[k] * PIECE // 4)]
        pltpu.make_async_remote_copy(
            src_ref=share,
            dst_ref=share,
            send_sem=send_sem.at[k],
            recv_sem=recv_a.at[0, 0, 0],
            device_id=sib,
            device_id_type=MESH,
        ).wait_send()


def on_device(
    amplitudes,
    dressing,
    integrals,
    occupied_energy,
    virtual_energy,
    occupied_rows,
    virtual_rows,
    occupied_columns,
    virtual_columns,
):
    anywhere = pl.BlockSpec(memory_space=pl.ANY)
    vmem = pl.BlockSpec(memory_space=pltpu.VMEM)
    smem = pl.BlockSpec(memory_space=pltpu.SMEM)
    residual = pl.pallas_call(
        kernel,
        out_shape=pltpu.VMEM((2, 1024, 1024), F32),
        in_specs=[anywhere, anywhere, anywhere, vmem, vmem, smem, vmem, smem, vmem],
        out_specs=vmem,
        scratch_shapes=[
            pltpu.VMEM((3, 2, 1024, 1024), F32),
            pltpu.VMEM((3, 1024, 1024), F32),
            pltpu.VMEM((3, 1024, 1024), BF16),
            pltpu.VMEM((3, 1024, 1024), BF16),
            pltpu.VMEM((1024, 128), F32),
            pltpu.VMEM((8, 1024), F32),
            pltpu.VMEM((8, 128), F32),
            pltpu.SemaphoreType.DMA((3,)),
            pltpu.SemaphoreType.DMA((3, 16)),
            pltpu.SemaphoreType.DMA((3, 2, 16)),
            pltpu.SemaphoreType.DMA((8,)),
            pltpu.SemaphoreType.DMA((8,)),
        ],
        compiler_params=pltpu.CompilerParams(
            collective_id=0, has_side_effects=True, vmem_limit_bytes=55 * 2**20
        ),
        cost_estimate=pl.CostEstimate(
            flops=42_000_000_000, bytes_accessed=20_000_000, transcendentals=0
        ),
    )(
        amplitudes,
        dressing,
        jnp.transpose(integrals, (1, 0, 2)),
        occupied_energy.reshape(1, -1),
        virtual_energy.reshape(1, -1),
        occupied_rows,
        virtual_rows.reshape(1, -1),
        occupied_columns,
        virtual_columns.reshape(1, -1),
    )
    return residual.reshape(2048, 1024)


def solution(mesh):
    return jax.shard_map(
        on_device,
        mesh=mesh,
        in_specs=(
            P("row", None, "col", None),
            P(),
            P("row", None, "col"),
            P(),
            P(),
            P("row"),
            P(),
            P("col"),
            P(),
        ),
        out_specs=P("row", "col"),
        check_vma=False,
    )
```
